256 devices in a mesh: row: 8 (over y_hi, x), col: 8 (over z), head: 4 (over y_lo, core).
Axes of the slice: x: 4, y: 4 (y_hi: 2, y_lo: 2; y = y_hi * 2 + y_lo), z: 8, core: 2. Of those that a mesh axis runs over, the one named last changes fastest.
Arguments:
- queries: bfloat16 [4, 32, 320, 1024], P('head', None, 'row', 'col'), may hold values from -6.5 to 6.5
- key_vectors: bfloat16 [4, 32, 320, 1024], P('head', None, 'row', 'col'), may hold values from -6.5 to 6.5
- value_vectors: bfloat16 [4, 32, 320, 1024], P('head', None, 'row', 'col'), may hold values from -6 to 6
- gate_logits: bfloat16 [4, 32, 320, 1024], P('head', None, 'row', 'col'), may hold values from -6 to 6
- cotangent: bfloat16 [4, 32, 320, 1024], P('head', None, 'row', 'col'), may hold values from -24 to 24
- pair_normed: bfloat16 [128, 1024, 1024], P('head', 'row', 'col'), may hold values from -6 to 6
- bias_weight: bfloat16 [128, 4], P('head'), may hold values from -0.75 to 0.75
- chain_lengths: int32 [8], replicated, may hold values from 51 to 128, as said below
Outputs:
- query_grad: bfloat16 [4, 32, 320, 1024], P('head', None, 'row', 'col')
- key_grad: bfloat16 [4, 32, 320, 1024], P('head', None, 'row', 'col')
- value_grad: bfloat16 [4, 32, 320, 1024], P('head', None, 'row', 'col')
- gate_grad: bfloat16 [4, 32, 320, 1024], P('head', None, 'row', 'col')
- pair_grad: bfloat16 [128, 1024, 1024], P('head', 'row', 'col')
The draws below stay inside these ranges and needn't reach their ends.
Inputs may be any that keep to these rules, and one draw needn't show every extreme that they name: `chain_lengths`: every chain has at least one token; positions from the sum of the lengths on are padding.
All inputs are finite; a program needn't handle non-finite values.
Results may differ from the reference program's by a relative error of at most 0.027.
Values may be sent and summed in bfloat16 or wider, within the bound.
No kernel may reach another device: no remote copies, remote signals or barrier semaphores. Data moves between devices by JAX's collectives and lax.ppermute only.
A program may use at most 128 MiB of HBM per device.

```python
import jax
import jax.numpy as jnp
from jax import lax

PAIR = 128
HEADS = 4
HEAD_DIM = 32
TOKENS = 1024
CHAINS = 8
ROWS = 320


def draw_queries(key, part):
    key = jax.random.fold_in(key, 11)
    values = jax.random.truncated_normal(key, -4.0, 4.0, (HEADS, HEAD_DIM, ROWS, TOKENS), jnp.float32)
    return values.astype(jnp.bfloat16)


def draw_key_vectors(key, part):
    key = jax.random.fold_in(key, 13)
    values = jax.random.truncated_normal(key, -4.0, 4.0, (HEADS, HEAD_DIM, ROWS, TOKENS), jnp.float32)
    return values.astype(jnp.bfloat16)


def draw_chain_lengths(key, part):
    key = jax.random.fold_in(key, 5)
    lengths = jax.random.randint(key, (CHAINS,), TOKENS // 20 + 1, TOKENS // 8, jnp.int32)
    order = jax.random.permutation(jax.random.fold_in(key, 1), CHAINS)
    lengths = lengths.at[order[0]].set(TOKENS // 8)
    lengths = lengths.at[order[1]].set(TOKENS // 20)
    return lengths


def steps_of(rng, extent, pieces, least, high):
    def one(dim, blocks):
        draws = jax.random.uniform(jax.random.fold_in(jax.random.fold_in(rng, 6), dim), (blocks,), jnp.float32, least / len(pieces), high / len(pieces))
        return jnp.repeat(jnp.exp(draws), extent[dim] // blocks).reshape((-1,) + (1,) * (len(extent) - dim - 1))

    loudness = one(*pieces[0])
    for cut in pieces[1:]:
        loudness = loudness * one(*cut)
    return loudness


def scatter_about(stream_key, shape, deviation, bound, cuts=(), kind=jnp.bfloat16):
    factor_of = steps_of(stream_key, shape, cuts, -0.22, 0.18) if cuts else 1.0
    result = jax.random.normal(stream_key, shape, jnp.float32) * deviation * factor_of
    return jnp.minimum(jnp.maximum(result, -bound), bound).astype(kind)


def setup_inputs(seed: int = 0) -> dict:
    arg_keys = jax.random.split(jax.random.key(seed), 9)
    return {
        "queries": draw_queries(jax.random.fold_in(arg_keys[8], 71), 0),
        "key_vectors": draw_key_vectors(jax.random.fold_in(arg_keys[8], 71), 0),
        "value_vectors": scatter_about(arg_keys[2], (HEADS, HEAD_DIM, ROWS, TOKENS), 1.0, 6.0, ((0, 4), (2, 8), (3, 8))),
        "gate_logits": scatter_about(arg_keys[3], (HEADS, HEAD_DIM, ROWS, TOKENS), 1.5, 6.0, ((0, 4), (2, 8), (3, 8))),
        "cotangent": scatter_about(arg_keys[4], (HEADS, HEAD_DIM, ROWS, TOKENS), 4.0, 24.0, ((0, 4), (2, 8), (3, 8))),
        "pair_normed": scatter_about(arg_keys[5], (PAIR, TOKENS, TOKENS), 1.0, 6.0, ((0, 4), (1, 8), (2, 8))),
        "bias_weight": scatter_about(arg_keys[6], (PAIR, HEADS), (PAIR // 2) ** -0.5, 0.75, ((0, 4),)),
        "chain_lengths": draw_chain_lengths(jax.random.fold_in(arg_keys[8], 71), 0),
    }


def round_bf16(source):
    return lax.optimization_barrier(source.astype(jnp.bfloat16)).astype(jnp.float32)


def reference(queries, key_vectors, value_vectors, gate_logits, cotangent, pair_normed, bias_weight, chain_lengths):
    score_scale = HEAD_DIM ** -0.5
    flat_pair = pair_normed.reshape(PAIR, TOKENS * TOKENS)
    bias = jnp.dot(bias_weight.T, flat_pair, preferred_element_type=jnp.float32).reshape(HEADS, TOKENS, TOKENS)
    token_count = jnp.sum(chain_lengths)
    live_keys = jnp.arange(TOKENS, dtype=jnp.int32) < token_count

    def one_row(bias_grad, row_index):
        query_row = lax.dynamic_index_in_dim(queries, row_index, 2, keepdims=False).astype(jnp.float32)
        key_row = lax.dynamic_index_in_dim(key_vectors, row_index, 2, keepdims=False).astype(jnp.float32)
        value_row = lax.dynamic_index_in_dim(value_vectors, row_index, 2, keepdims=False).astype(jnp.float32)
        gate_row = lax.dynamic_index_in_dim(gate_logits, row_index, 2, keepdims=False).astype(jnp.float32)
        grad_row = lax.dynamic_index_in_dim(cotangent, row_index, 2, keepdims=False).astype(jnp.float32)
        scores = jnp.einsum('hdj,hdk->hjk', query_row, key_row) * score_scale + bias
        scores = jnp.where(live_keys[None, None, :], scores, -1e9)
        row_max = jnp.max(scores, axis=-1, keepdims=True)
        weights = jnp.exp(scores - row_max)
        attention = weights / jnp.sum(weights, axis=-1, keepdims=True)
        attention_b = round_bf16(attention)
        attended = jnp.einsum('hjk,hdk->hdj', attention_b, value_row)
        gate = jax.nn.sigmoid(gate_row)
        gate_grad = (grad_row * attended * gate * (1.0 - gate)).astype(jnp.bfloat16)
        attended_grad = round_bf16(grad_row * gate)
        prob_grad = jnp.einsum('hdj,hdk->hjk', attended_grad, value_row)
        row_delta = jnp.sum(attended_grad * attended, axis=1)
        score_grad = attention * (prob_grad - row_delta[:, :, None])
        score_grad_b = round_bf16(score_grad)
        query_grad = (jnp.einsum('hjk,hdk->hdj', score_grad_b, key_row) * score_scale).astype(jnp.bfloat16)
        key_grad = (jnp.einsum('hjk,hdj->hdk', score_grad_b, query_row) * score_scale).astype(jnp.bfloat16)
        value_grad = jnp.einsum('hjk,hdj->hdk', attention_b, attended_grad).astype(jnp.bfloat16)
        return bias_grad + score_grad, (query_grad, key_grad, value_grad, gate_grad)

    start_grad = jnp.zeros((HEADS, TOKENS, TOKENS), jnp.float32)
    bias_grad, stacked = lax.scan(one_row, start_grad, jnp.arange(ROWS, dtype=jnp.int32))
    query_grad, key_grad, value_grad, gate_grad = [jnp.moveaxis(item, 0, 2) for item in stacked]
    pair_grad = jnp.dot(bias_weight.astype(jnp.float32), bias_grad.reshape(HEADS, TOKENS * TOKENS), precision=lax.Precision.HIGHEST)
    pair_grad = pair_grad.reshape(PAIR, TOKENS, TOKENS).astype(jnp.bfloat16)
    return (query_grad, key_grad, value_grad, gate_grad, pair_grad)
```

```python
import functools
import math

import jax
import jax.numpy as jnp
from jax import lax
from jax.experimental import pallas as pl
from jax.experimental.pallas import tpu as pltpu
from jax.sharding import PartitionSpec as P

HEADS = 4
DIM = 32
BLK = 128
SCALE = DIM**-0.5
LOG2E = math.log2(math.e)
BF = jnp.bfloat16
F32 = jnp.float32
NT = (((1,), (1,)), ((), ()))
NEG = -1e9


def split_kernel(meta_ref, q_ref, k_ref, v_ref, g_ref, c_ref, out_ref, buf):
    col = meta_ref[0]
    cols = out_ref.shape[0]
    per = out_ref.shape[1]
    rows = q_ref.shape[2]
    ag = (c_ref[0].astype(F32) * jax.nn.sigmoid(g_ref[0].astype(F32))).astype(BF)
    for a, value in enumerate((q_ref[0], k_ref[0], v_ref[0], ag)):
        buf[a] = value.astype(F32).reshape(DIM * rows, BLK)
    for dest in range(cols):
        slot = lax.rem(dest - col + cols, cols)
        for r in range(per):
            for a in range(4):
                out_ref[slot, r, a] = buf[a, pl.ds(r * cols + dest, DIM, rows)].astype(BF)


def merge_kernel(meta_ref, x_ref, g_ref, c_ref, dq_ref, dk_ref, dv_ref, dg_ref, buf):
    col = meta_ref[0]
    cols = x_ref.shape[0]
    per = x_ref.shape[1]
    rows = dq_ref.shape[2]
    for src in range(cols):
        slot = lax.rem(src - col + cols, cols)
        for r in range(per):
            for a in range(4):
                buf[a, pl.ds(r * cols + src, DIM, rows)] = x_ref[slot, r, a].astype(F32)
    for a, out in enumerate((dq_ref, dk_ref, dv_ref)):
        out[0] = buf[a].reshape(DIM, rows, BLK).astype(BF)
    gate = jax.nn.sigmoid(g_ref[0].astype(F32))
    attended = buf[3].reshape(DIM, rows, BLK)
    dg_ref[0] = (c_ref[0].astype(F32) * attended * gate * (1.0 - gate)).astype(BF)


def attend_kernel(
    meta_ref, x_ref, b_ref, y_ref, db_ref, ka, vta, va, kk, s_ref, p_ref, acc, dbacc
):
    cols = x_ref.shape[0]
    row = pl.program_id(0)
    col = meta_ref[0]
    count = meta_ref[1]

    @pl.when(row == 0)
    def _():
        dbacc[...] = jnp.zeros_like(dbacc)

    acc[...] = jnp.zeros_like(acc)
    ones16 = jnp.ones((16, BLK), BF)
    zeros48 = jnp.zeros((48, BLK), BF)
    lane = lax.broadcasted_iota(jnp.int32, (16, BLK), 1)
    for s in range(cols):
        at = pl.ds(s * BLK, BLK)
        key = x_ref[s, 0, 1]
        val = x_ref[s, 0, 2]
        first = lax.rem(col - s + cols, cols) * BLK
        mask = jnp.where(first + lane < count, 0.0, NEG).astype(BF)
        ka[at, :] = jnp.concatenate([key, key, mask, zeros48], 0).T
        vta[at, :] = jnp.concatenate([val, val, ones16, zeros48], 0).T
        va[0:DIM, at] = val
        va[DIM : DIM + 16, at] = ones16
        kk[:, at] = key
    sub = lax.broadcasted_iota(jnp.int32, (16, 2 * BLK), 0)
    unit = jnp.where(sub == 0, 1.0, 0.0).astype(BF)
    zero48 = jnp.zeros((48, 2 * BLK), BF)
    zero64 = jnp.zeros((64, 2 * BLK), BF)
    zero32 = jnp.zeros((32, 2 * BLK), BF)

    def chunk(jc, carry):
        j0 = 2 * jc
        j1 = j0 + 1
        slot0 = meta_ref[2 + j0]
        slot1 = meta_ref[2 + j1]
        q = jnp.concatenate([x_ref[j0, 0, 0], x_ref[j1, 0, 0]], 1)
        ag = jnp.concatenate([x_ref[j0, 0, 3], x_ref[j1, 0, 3]], 1).astype(F32)
        qs = q.astype(F32) * (SCALE * LOG2E)
        qhi = qs.astype(BF)
        qlo = (qs - qhi.astype(F32)).astype(BF)
        qa = jnp.concatenate([qhi, qlo, unit, zero48], 0)
        top = None
        for kb in range(cols // 2):
            at = pl.ds(kb * 2 * BLK, 2 * BLK)
            s = jnp.dot(ka[at, :], qa, preferred_element_type=F32)
            bias = jnp.concatenate(
                [
                    jnp.concatenate([b_ref[slot0, 2 * kb + e], b_ref[slot1, 2 * kb + e]], 1)
                    for e in range(2)
                ],
                0,
            )
            s = s + bias.astype(F32)
            s_ref[at, :] = s
            m = jnp.max(s, axis=0, keepdims=True)
            top = m if top is None else jnp.maximum(top, m)
        o = None
        for kb in range(cols // 2):
            at = pl.ds(kb * 2 * BLK, 2 * BLK)
            p = jnp.exp2(s_ref[at, :] - top)
            s_ref[at, :] = p
            pb = p.astype(BF)
            p_ref[at, :] = pb
            part = jnp.dot(va[:, at], pb, preferred_element_type=F32)
            o = part if o is None else o + part
        inv = 1.0 / o[DIM : DIM + 1]
        att = o[:DIM] * inv
        delta = jnp.sum(ag * att, axis=0, keepdims=True) * inv
        do = ag * inv
        dohi = do.astype(BF)
        dolo = (do - dohi.astype(F32)).astype(BF)
        d1 = delta.astype(BF).astype(F32)
        d2 = (delta - d1).astype(BF).astype(F32)
        d3 = delta - d1 - d2
        drow = jnp.where(sub == 0, -d1, jnp.where(sub == 1, -d2, jnp.where(sub == 2, -d3, 0.0)))
        doa = jnp.concatenate([dohi, dolo, drow.astype(BF), zero48], 0)
        w = jnp.concatenate(
            [
                jnp.concatenate([dohi, dolo, zero64], 0),
                jnp.concatenate([zero64, q, zero32], 0),
            ],
            1,
        )
        dq = None
        for kb in range(cols // 2):
            at = pl.ds(kb * 2 * BLK, 2 * BLK)
            t = jnp.dot(vta[at, :], doa, preferred_element_type=F32)
            ds = s_ref[at, :] * t
            dsb = ds.astype(BF)
            for e in range(2):
                part = ds[e * BLK : (e + 1) * BLK]
                dbacc[slot0, 2 * kb + e] += part[:, :BLK]
                dbacc[slot1, 2 * kb + e] += part[:, BLK:]
            part = jnp.dot(kk[:, at], dsb, preferred_element_type=F32)
            dq = part if dq is None else dq + part
            both = jnp.concatenate([p_ref[at, :], dsb], 1)
            acc[at, :] += lax.dot_general(both, w, NT, preferred_element_type=F32)
        dq = (dq * SCALE).astype(BF)
        attb = att.astype(BF)
        y_ref[j0, 0, 0] = dq[:, :BLK]
        y_ref[j1, 0, 0] = dq[:, BLK:]
        y_ref[j0, 0, 3] = attb[:, :BLK]
        y_ref[j1, 0, 3] = attb[:, BLK:]
        return carry

    lax.fori_loop(0, cols // 2, chunk, 0)
    for s in range(cols):
        a = acc[s * BLK : (s + 1) * BLK, :].T
        y_ref[s, 0, 2] = (a[0:DIM] + a[DIM : 2 * DIM]).astype(BF)
        y_ref[s, 0, 1] = (a[2 * DIM : 3 * DIM] * SCALE).astype(BF)

    @pl.when(row == pl.num_programs(0) - 1)
    def _():
        db_ref[...] = dbacc[...].astype(BF)


def attend(meta, x, bias):
    cols, rows = x.shape[:2]
    slots = bias.shape[0]
    wide = cols * BLK
    return pl.pallas_call(
        attend_kernel,
        grid=(rows,),
        in_specs=[
            pl.BlockSpec(memory_space=pltpu.SMEM),
            pl.BlockSpec((cols, 1, 4, DIM, BLK), lambda r: (0, r, 0, 0, 0)),
            pl.BlockSpec((slots, cols, BLK, BLK), lambda r: (0, 0, 0, 0)),
        ],
        out_specs=[
            pl.BlockSpec((cols, 1, 4, DIM, BLK), lambda r: (0, r, 0, 0, 0)),
            pl.BlockSpec((slots, cols, BLK, BLK), lambda r: (0, 0, 0, 0)),
        ],
        out_shape=[
            jax.ShapeDtypeStruct(x.shape, BF),
            jax.ShapeDtypeStruct(bias.shape, BF),
        ],
        scratch_shapes=[
            pltpu.VMEM((wide, BLK), BF),
            pltpu.VMEM((wide, BLK), BF),
            pltpu.VMEM((DIM + 16, wide), BF),
            pltpu.VMEM((DIM, wide), BF),
            pltpu.VMEM((wide, 2 * BLK), F32),
            pltpu.VMEM((wide, 2 * BLK), BF),
            pltpu.VMEM((wide, BLK), F32),
            pltpu.VMEM((slots, cols, BLK, BLK), F32),
        ],
        compiler_params=pltpu.CompilerParams(vmem_limit_bytes=40 * 1024 * 1024),
    )(meta, x, bias)


SMEM_SPEC = pl.BlockSpec(memory_space=pltpu.SMEM)
VMEM_SPEC = pl.BlockSpec(memory_space=pltpu.VMEM)


def split(meta, q, k, v, g, c, cols):
    rows = q.shape[2]
    return pl.pallas_call(
        split_kernel,
        in_specs=[SMEM_SPEC] + [VMEM_SPEC] * 5,
        out_specs=VMEM_SPEC,
        out_shape=jax.ShapeDtypeStruct((cols, rows // cols, 4, DIM, BLK), BF),
        scratch_shapes=[pltpu.VMEM((4, DIM * rows, BLK), F32)],
        compiler_params=pltpu.CompilerParams(vmem_limit_bytes=24 * 1024 * 1024),
    )(meta, q, k, v, g, c)


def merge(meta, x, g, c):
    rows = g.shape[2]
    return pl.pallas_call(
        merge_kernel,
        in_specs=[SMEM_SPEC] + [VMEM_SPEC] * 3,
        out_specs=[VMEM_SPEC] * 4,
        out_shape=[jax.ShapeDtypeStruct(g.shape, BF)] * 4,
        scratch_shapes=[pltpu.VMEM((4, DIM * rows, BLK), F32)],
        compiler_params=pltpu.CompilerParams(vmem_limit_bytes=24 * 1024 * 1024),
    )(meta, x, g, c)


def shift(x, axis, n, by):
    return lax.ppermute(x, axis, [(i, (i + by) % n) for i in range(n)])


def shift_x(x, by):
    return lax.ppermute(x, "row", [(r, r // 4 * 4 + (r + by) % 4) for r in range(8)])


def swap_y(x):
    return lax.ppermute(x, "row", [(r, (r + 4) % 8) for r in range(8)])


def body(q, k, v, g, c, pair, weight, lengths):
    cols = lax.axis_size("col")
    col = lax.axis_index("col")
    row = lax.axis_index("row")
    head = lax.axis_index("head")
    count = jnp.sum(lengths)
    blocks = jnp.remainder(col - jnp.arange(cols), cols)
    slots = jnp.where(row // 4 == blocks // 4, 0, 4) + jnp.remainder(row - blocks, 4)
    meta = jnp.concatenate([jnp.stack([col, count]), slots]).astype(jnp.int32)

    partial = jnp.dot(
        weight.T, pair.reshape(pair.shape[0], BLK * BLK), preferred_element_type=F32
    ).reshape(HEADS, BLK, BLK)
    own = lax.dynamic_index_in_dim(partial, head, 0, keepdims=False)
    for s in range(1, HEADS):
        give = lax.dynamic_index_in_dim(
            partial, jnp.remainder(head + s, HEADS), 0, keepdims=False
        )
        own = own + shift(give, "head", HEADS, s)
    own = (own.T * LOG2E).astype(BF)

    x = split(meta, q, k, v, g, c, cols)
    pieces = [x[0]] + [shift(x[s], "col", cols, s) for s in range(1, cols)]

    along_z = jnp.stack([own] + [shift(own, "col", cols, s) for s in range(1, cols)])
    along_x = jnp.stack([along_z] + [shift_x(along_z, t) for t in range(1, 4)])
    bias = jnp.concatenate([along_x, swap_y(along_x)])

    y, db = attend(meta, jnp.stack(pieces), bias)

    z = jnp.stack([y[0]] + [shift(y[s], "col", cols, -s) for s in range(1, cols)])
    dq, dk, dv, dg = merge(meta, z, g, c)

    half = db[:4].astype(F32) + swap_y(db[4:]).astype(F32)
    halfb = half.astype(BF)
    quarter = half[0]
    for t in range(1, 4):
        quarter = quarter + shift_x(halfb[t], -t).astype(F32)
    quarterb = quarter.astype(BF)
    mine = quarter[0]
    for s in range(1, cols):
        mine = mine + shift(quarterb[s], "col", cols, -s).astype(F32)
    mine = mine.T
    wf = weight.astype(F32)
    every = [mine] + [shift(mine, "head", HEADS, s) for s in range(1, HEADS)]
    order = jnp.remainder(head - jnp.arange(HEADS), HEADS)
    turned = jnp.take(wf, order, axis=1)
    dpair = jnp.dot(
        turned,
        jnp.stack(every).reshape(HEADS, BLK * BLK),
        precision=lax.Precision.HIGHEST,
    )
    dpair = dpair.reshape(pair.shape).astype(BF)
    return dq, dk, dv, dg, dpair


def solution(mesh):
    spec = P("head", None, "row", "col")
    pair_spec = P("head", "row", "col")
    return jax.shard_map(
        body,
        mesh=mesh,
        in_specs=(spec,) * 5 + (pair_spec, P("head", None), P()),
        out_specs=(spec,) * 4 + (pair_spec,),
        check_vma=False,
    )
```

```python
import functools
import math

import jax
import jax.numpy as jnp
from jax import lax
from jax.experimental import pallas as pl
from jax.experimental.pallas import tpu as pltpu
from jax.sharding import PartitionSpec as P

HEADS = 4
DIM = 32
BLK = 128
SCALE = DIM**-0.5
LOG2E = math.log2(math.e)
BF = jnp.bfloat16
F32 = jnp.float32
NT = (((1,), (1,)), ((), ()))
NEG = -1e9


def split_kernel(q_ref, k_ref, v_ref, g_ref, c_ref, x_ref, buf):
    cols, per = x_ref.shape[:2]
    rows = q_ref.shape[2]
    ag = (c_ref[0].astype(F32) * jax.nn.sigmoid(g_ref[0].astype(F32))).astype(BF)
    for a, value in enumerate((q_ref[0], k_ref[0], v_ref[0], ag)):
        buf[a] = value.astype(F32).reshape(DIM * rows, BLK)
    for dest in range(cols):
        for r in range(per):
            for a in range(4):
                part = buf[a, pl.ds(r * cols + dest, DIM, rows)].astype(BF)
                x_ref[dest, r, a] = part


def merge_kernel(y_ref, z_ref, g_ref, c_ref, dq_ref, dk_ref, dv_ref, dg_ref, buf):
    cols, per = y_ref.shape[:2]
    rows = dq_ref.shape[2]
    for src in range(cols):
        for r in range(per):
            for a in range(4):
                part = z_ref[src, r, a - 1] if a in (1, 2) else y_ref[src, r, a // 3]
                buf[a, pl.ds(r * cols + src, DIM, rows)] = part.astype(F32)
    for a, out in enumerate((dq_ref, dk_ref, dv_ref)):
        out[0] = buf[a].reshape(DIM, rows, BLK).astype(BF)
    gate = jax.nn.sigmoid(g_ref[0].astype(F32))
    attended = buf[3].reshape(DIM, rows, BLK)
    dg_ref[0] = (c_ref[0].astype(F32) * attended * gate * (1.0 - gate)).astype(BF)


def attend_kernel(ts, first, last, extra, *refs):
    refs = list(refs)
    take = lambda n: [refs.pop(0) for _ in range(n)]
    meta_ref, x_ref = take(2)
    b_refs = take(len(ts))
    if first:
        ka_in = vta_in = acc_in = y_in = None
    else:
        ka_in, vta_in, acc_in, y_in = take(4)
    r_refs = take(extra)
    (y_ref,) = take(1)
    z_ref = take(1)[0] if last else None
    db_refs = take(len(ts))
    if last:
        ka_out = vta_out = None
        acc_out = None
    else:
        ka_out, vta_out, acc_out = take(3)
    ka, vta, va, kk, s_ref, p_ref, acc, dbacc = refs
    cols = x_ref.shape[0]
    row = pl.program_id(0)
    count = meta_ref[0]
    place = lambda s: lax.rem(meta_ref[9] - s + cols, cols)

    @pl.when(row == 0)
    def _():
        dbacc[...] = jnp.zeros_like(dbacc)

    ones16 = jnp.ones((16, BLK), BF)
    zeros48 = jnp.zeros((48, BLK), BF)
    lane = lax.broadcasted_iota(jnp.int32, (16, BLK), 1)
    for s in range(cols):
        at = pl.ds(s * BLK, BLK)
        key = x_ref[s, 0, 1]
        val = x_ref[s, 0, 2]
        if first:
            mask = jnp.where(s * BLK + lane < count, 0.0, NEG).astype(BF)
            ka[at, :] = jnp.concatenate([key, key, mask, zeros48], 0).T
            vta[at, :] = jnp.concatenate([val, val, ones16, zeros48], 0).T
        va[0:DIM, at] = val
        va[DIM : DIM + 16, at] = ones16
        kk[:, at] = key
    if first:
        acc[...] = jnp.zeros_like(acc)
        ka_use, vta_use = ka, vta
    else:
        acc[...] = acc_in[0]
        y_ref[...] = y_in[...]
        ka_use, vta_use = ka_in.at[0], vta_in.at[0]
    if not last:
        ka_out[0] = ka_use[...]
        vta_out[0] = vta_use[...]
    sub = lax.broadcasted_iota(jnp.int32, (16, 2 * BLK), 0)
    unit = jnp.where(sub == 0, 1.0, 0.0).astype(BF)
    zero48 = jnp.zeros((48, 2 * BLK), BF)
    zero64 = jnp.zeros((64, 2 * BLK), BF)
    zero32 = jnp.zeros((32, 2 * BLK), BF)

    def scores(n, t, steps):
        b_ref = b_refs[n]
        j0 = meta_ref[1 + 2 * t]
        j1 = meta_ref[2 + 2 * t]
        q = jnp.concatenate([x_ref[j0, 0, 0], x_ref[j1, 0, 0]], 1)
        qs = q.astype(F32) * (SCALE * LOG2E)
        qhi = qs.astype(BF)
        qlo = (qs - qhi.astype(F32)).astype(BF)
        qa = jnp.concatenate([qhi, qlo, unit, zero48], 0)
        top = None
        for kb in range(steps):
            at = pl.ds(kb * 2 * BLK, 2 * BLK)
            s = jnp.dot(ka_use[at, :], qa, preferred_element_type=F32)
            bias = jnp.concatenate(
                [
                    jnp.concatenate([b_ref[0, place(2 * kb + e)], b_ref[1, place(2 * kb + e)]], 1)
                    for e in range(2)
                ],
                0,
            )
            s = s + bias
            s_ref[n, at, :] = s
            m = jnp.max(s, axis=0, keepdims=True)
            top = m if top is None else jnp.maximum(top, m)
        return j0, j1, q, top

    def weights(n, top, steps):
        o = None
        for kb in range(steps):
            at = pl.ds(kb * 2 * BLK, 2 * BLK)
            p = jnp.exp2(s_ref[n, at, :] - top)
            s_ref[n, at, :] = p
            pb = p.astype(BF)
            p_ref[n, at, :] = pb
            part = jnp.dot(va[:, at], pb, preferred_element_type=F32)
            o = part if o is None else o + part
        return o

    def middle(n, j0, j1, q, o):
        ag = jnp.concatenate([x_ref[j0, 0, 3], x_ref[j1, 0, 3]], 1).astype(F32)
        inv = 1.0 / o[DIM : DIM + 1]
        att = o[:DIM] * inv
        delta = jnp.sum(ag * att, axis=0, keepdims=True) * inv
        do = ag * inv
        dohi = do.astype(BF)
        dolo = (do - dohi.astype(F32)).astype(BF)
        d1 = delta.astype(BF).astype(F32)
        d2 = (delta - d1).astype(BF).astype(F32)
        d3 = delta - d1 - d2
        drow = jnp.where(sub == 0, -d1, jnp.where(sub == 1, -d2, jnp.where(sub == 2, -d3, 0.0)))
        doa = jnp.concatenate([dohi, dolo, drow.astype(BF), zero48], 0)
        w = jnp.concatenate(
            [
                jnp.concatenate([dohi, dolo, zero64], 0),
                jnp.concatenate([zero64, q, zero32], 0),
            ],
            1,
        )
        attb = att.astype(BF)
        y_ref[j0, 0, 1] = attb[:, :BLK]
        y_ref[j1, 0, 1] = attb[:, BLK:]
        return doa, w

    def gradients(n, kb, doa):
        at = pl.ds(kb * 2 * BLK, 2 * BLK)
        dp = jnp.dot(vta_use[at, :], doa, preferred_element_type=F32)
        ds = s_ref[n, at, :] * dp
        dsb = ds.astype(BF)
        for e in range(2):
            part = ds[e * BLK : (e + 1) * BLK]
            dbacc[n, 0, place(2 * kb + e)] += part[:, :BLK]
            dbacc[n, 1, place(2 * kb + e)] += part[:, BLK:]
        both = jnp.concatenate([p_ref[n, at, :], dsb], 1)
        return jnp.dot(kk[:, at], dsb, preferred_element_type=F32), both

    def chunks(some, steps):
        first_stage = [scores(n, ts[n], steps) for n in some]
        outs = [weights(n, f[3], steps) for n, f in zip(some, first_stage)]
        mids = [middle(n, f[0], f[1], f[2], o) for n, f, o in zip(some, first_stage, outs)]
        dqs = [None] * len(some)
        for kb in range(steps):
            at = pl.ds(kb * 2 * BLK, 2 * BLK)
            terms = []
            for i, n in enumerate(some):
                part, both = gradients(n, kb, mids[i][0])
                dqs[i] = part if dqs[i] is None else dqs[i] + part
                terms.append(lax.dot_general(both, mids[i][1], NT, preferred_element_type=F32))
            acc[at, :] += sum(terms[1:], terms[0])
        for f, dq in zip(first_stage, dqs):
            dq = (dq * SCALE).astype(BF)
            y_ref[f[0], 0, 0] = dq[:, :BLK]
            y_ref[f[1], 0, 0] = dq[:, BLK:]

    def live(steps, low, high):
        @pl.when(jnp.logical_and(count > low, count <= high))
        def _():
            for start in range(0, len(ts), 2):
                chunks(range(start, min(start + 2, len(ts))), steps)

    full = cols // 2
    live(full, (full - 1) * 2 * BLK, full * 2 * BLK)
    live(full - 1, (full - 2) * 2 * BLK, (full - 1) * 2 * BLK)
    live(full - 2, 0, (full - 2) * 2 * BLK)

    if last:
        for s in range(cols):
            a = acc[s * BLK : (s + 1) * BLK, :].T
            z_ref[s, 0, 1] = (a[0:DIM] + a[DIM : 2 * DIM]).astype(BF)
            z_ref[s, 0, 0] = (a[2 * DIM : 3 * DIM] * SCALE).astype(BF)
    else:
        acc_out[0] = acc[...]

    @pl.when(row == pl.num_programs(0) - 1)
    def _():
        for n in range(len(ts)):
            total = dbacc[n]
            if n == len(ts) - 1:
                for r_ref in r_refs:
                    total = total + r_ref[...].astype(F32)
            db_refs[n][...] = total.astype(db_refs[n].dtype)


def attend(meta, x, biases, ts, state=None, last=False, extra=()):
    first = state is None
    cols, rows = x.shape[:2]
    wide = cols * BLK
    per_row = lambda n: pl.BlockSpec((cols, 1, n, DIM, BLK), lambda r: (0, r, 0, 0, 0))
    pairs = jax.ShapeDtypeStruct((cols, rows, 2, DIM, BLK), BF)
    tile = pl.BlockSpec((2, cols, BLK, BLK), lambda r: (0, 0, 0, 0))
    flat = pl.BlockSpec((1, wide, BLK), lambda r: (r, 0, 0))
    tile_shape = (2, cols, BLK, BLK)
    flat_shape = (rows, wide, BLK)
    in_specs = [pl.BlockSpec(memory_space=pltpu.SMEM), per_row(4)] + [tile] * len(ts)
    operands = [meta, x] + [biases[t] for t in ts]
    if not first:
        in_specs += [flat, flat, flat, per_row(2)]
        operands += list(state)
    in_specs += [tile] * len(extra)
    operands += list(extra)
    out_specs = [per_row(2)] * (2 if last else 1) + [tile] * len(ts)
    out_shape = [pairs] * (2 if last else 1)
    out_shape += [jax.ShapeDtypeStruct(tile_shape, F32 if last else BF)] * len(ts)
    if not last:
        out_specs += [flat] * 3
        out_shape += [jax.ShapeDtypeStruct(flat_shape, dt) for dt in (BF, BF, F32)]
    outs = pl.pallas_call(
        functools.partial(attend_kernel, ts, first, last, len(extra)),
        grid=(rows,),
        in_specs=in_specs,
        out_specs=out_specs,
        out_shape=out_shape,
        scratch_shapes=[
            pltpu.VMEM((wide, BLK), BF),
            pltpu.VMEM((wide, BLK), BF),
            pltpu.VMEM((DIM + 16, wide), BF),
            pltpu.VMEM((DIM, wide), BF),
            pltpu.VMEM((len(ts), wide, 2 * BLK), F32),
            pltpu.VMEM((len(ts), wide, 2 * BLK), BF),
            pltpu.VMEM((wide, BLK), F32),
            pltpu.VMEM((len(ts),) + tile_shape, F32),
        ],
        compiler_params=pltpu.CompilerParams(vmem_limit_bytes=32 * 1024 * 1024),
        cost_estimate=pl.CostEstimate(
            flops=len(ts) * 2_000_000_000, bytes_accessed=8_000_000, transcendentals=0
        ),
    )(*operands)
    if last:
        return *outs[:2], dict(zip(ts, outs[2:])), None
    dbs, rest = outs[1 : 1 + len(ts)], outs[1 + len(ts) :]
    return outs[0], dict(zip(ts, dbs)), (*rest, outs[0])


VMEM_SPEC = pl.BlockSpec(memory_space=pltpu.VMEM)


def split(q, k, v, g, c, cols):
    rows = q.shape[2]
    return pl.pallas_call(
        split_kernel,
        in_specs=[VMEM_SPEC] * 5,
        out_specs=VMEM_SPEC,
        out_shape=jax.ShapeDtypeStruct((cols, rows // cols, 4, DIM, BLK), BF),
        scratch_shapes=[pltpu.VMEM((4, DIM * rows, BLK), F32)],
        compiler_params=pltpu.CompilerParams(vmem_limit_bytes=24 * 1024 * 1024),
    )(q, k, v, g, c)


def merge(y, z, g, c):
    rows = g.shape[2]
    return pl.pallas_call(
        merge_kernel,
        in_specs=[VMEM_SPEC] * 4,
        out_specs=[VMEM_SPEC] * 4,
        out_shape=[jax.ShapeDtypeStruct(g.shape, BF)] * 4,
        scratch_shapes=[pltpu.VMEM((4, DIM * rows, BLK), F32)],
        compiler_params=pltpu.CompilerParams(vmem_limit_bytes=24 * 1024 * 1024),
    )(y, z, g, c)


def shift(x, axis, n, by):
    return lax.ppermute(x, axis, [(i, (i + by) % n) for i in range(n)])


def shift_x(x, by):
    return lax.ppermute(x, "row", [(r, r // 4 * 4 + (r + by) % 4) for r in range(8)])


def swap_y(x):
    return lax.ppermute(x, "row", [(r, (r + 4) % 8) for r in range(8)])


def gather_z(own, cols):
    far = jnp.stack([own, shift(own, "col", cols, 3), shift(own, "col", cols, -3)])
    low = shift(far, "col", cols, 1)
    high = shift(far[:2], "col", cols, -1)
    return jnp.stack([own, low[0], high[1], far[1], low[1], far[2], low[2], high[0]])


def reduce_z(strip, cols, after):
    part = strip.astype(BF)
    low = shift(jnp.stack([part[1], part[4], part[6]]), "col", cols, -1).astype(F32)
    high = shift(jnp.stack([part[7], part[2]]), "col", cols, 1).astype(F32)
    low, high, after = lax.optimization_barrier((low, high, after))
    left = shift((strip[3] + low[1] + high[1]).astype(BF), "col", cols, -3).astype(F32)
    right = shift((strip[5] + low[2]).astype(BF), "col", cols, 3).astype(F32)
    return strip[0] + low[0] + high[0] + left + right, after


def body(q, k, v, g, c, pair, weight, lengths):
    cols = lax.axis_size("col")
    col = lax.axis_index("col")
    row = lax.axis_index("row")
    head = lax.axis_index("head")
    count = jnp.sum(lengths)
    away = jnp.arange(8)
    block = jnp.remainder(row // 4 + away % 2, 2) * 4 + jnp.remainder(row - away // 2, 4)
    meta = jnp.concatenate([count[None], block, col[None]]).astype(jnp.int32)

    partial = jnp.dot(
        weight.T, pair.reshape(pair.shape[0], BLK * BLK), preferred_element_type=F32
    ).reshape(HEADS, BLK, BLK)
    own = lax.dynamic_index_in_dim(partial, head, 0, keepdims=False)
    for s in range(1, HEADS):
        give = lax.dynamic_index_in_dim(
            partial, jnp.remainder(head + s, HEADS), 0, keepdims=False
        )
        own = own + shift(give, "head", HEADS, s)
    own = (own.T * LOG2E).astype(jnp.float16)

    x = split(q, k, v, g, c, cols)
    along_z = gather_z(own, cols)
    x, along_z = lax.optimization_barrier((x, along_z))
    x = lax.all_to_all(x, "col", 0, 0)
    along_y = jnp.stack([along_z, swap_y(along_z)])
    raw = {t: shift_x(along_y, t) for t in (2, 1, 3)}

    _, db, state = attend(meta, x, {2: raw[2].astype(F32)}, (2,))
    got2 = shift_x(db[2], -2)
    raw1, raw3, state = lax.optimization_barrier((raw[1], raw[3], state))
    _, db, state = attend(meta, x, {1: raw1.astype(F32), 3: raw3.astype(F32)}, (1, 3), state)
    got1, got3 = shift_x(db[1], -1), shift_x(db[3], -3)
    y, z, db, _ = attend(meta, x, {0: along_y.astype(F32)}, (0,), state, True, (got2,))

    y = lax.all_to_all(y, "col", 0, 0)
    both = db[0] + got1.astype(F32) + got3.astype(F32)
    strip = both[0] + swap_y(both[1].astype(BF)).astype(F32)
    mine, z = reduce_z(strip, cols, z)
    z = lax.all_to_all(z, "col", 0, 0)
    dq, dk, dv, dg = merge(y, z, g, c)
    mine = mine.T
    wf = weight.astype(F32)
    every = [mine] + [shift(mine, "head", HEADS, s) for s in range(1, HEADS)]
    order = jnp.remainder(head - jnp.arange(HEADS), HEADS)
    turned = jnp.take(wf, order, axis=1)
    dpair = jnp.dot(
        turned,
        jnp.stack(every).reshape(HEADS, BLK * BLK),
        precision=lax.Precision.HIGHEST,
    )
    dpair = dpair.reshape(pair.shape).astype(BF)
    return dq, dk, dv, dg, dpair


def solution(mesh):
    spec = P("head", None, "row", "col")
    pair_spec = P("head", "row", "col")
    return jax.shard_map(
        body,
        mesh=mesh,
        in_specs=(spec,) * 5 + (pair_spec, P("head", None), P()),
        out_specs=(spec,) * 4 + (pair_spec,),
        check_vma=False,
    )
```

```python
import functools
import math

import jax
import jax.numpy as jnp
from jax import lax
from jax.experimental import pallas as pl
from jax.experimental.pallas import tpu as pltpu
from jax.sharding import PartitionSpec as P

HEADS = 4
DIM = 32
BLK = 128
SCALE = DIM**-0.5
LOG2E = math.log2(math.e)
BF = jnp.bfloat16
F32 = jnp.float32
NT = (((1,), (1,)), ((), ()))
NEG = -1e9


def split_kernel(q_ref, k_ref, v_ref, g_ref, c_ref, x_ref, buf):
    cols, per = x_ref.shape[:2]
    rows = q_ref.shape[2]
    ag = (c_ref[0].astype(F32) * jax.nn.sigmoid(g_ref[0].astype(F32))).astype(BF)
    for a, value in enumerate((q_ref[0], k_ref[0], v_ref[0], ag)):
        buf[a] = value.astype(F32).reshape(DIM * rows, BLK)
    for dest in range(cols):
        for r in range(per):
            for a in range(4):
                part = buf[a, pl.ds(r * cols + dest, DIM, rows)].astype(BF)
                x_ref[dest, r, a] = part


def merge_kernel(y_ref, z_ref, g_ref, c_ref, dq_ref, dk_ref, dv_ref, dg_ref, buf):
    cols, per = y_ref.shape[:2]
    rows = dq_ref.shape[2]
    for src in range(cols):
        for r in range(per):
            for a in range(4):
                part = z_ref[src, r, a - 1] if a in (1, 2) else y_ref[src, r, a // 3]
                buf[a, pl.ds(r * cols + src, DIM, rows)] = part.astype(F32)
    for a, out in enumerate((dq_ref, dk_ref, dv_ref)):
        out[0] = buf[a].reshape(DIM, rows, BLK).astype(BF)
    gate = jax.nn.sigmoid(g_ref[0].astype(F32))
    attended = buf[3].reshape(DIM, rows, BLK)
    dg_ref[0] = (c_ref[0].astype(F32) * attended * gate * (1.0 - gate)).astype(BF)


def attend_kernel(ts, first, last, extra, *refs):
    refs = list(refs)
    take = lambda n: [refs.pop(0) for _ in range(n)]
    meta_ref, x_ref = take(2)
    b_refs = take(len(ts))
    if first:
        ka_in = vta_in = acc_in = y_in = None
    else:
        ka_in, vta_in, acc_in, y_in = take(4)
    r_refs = take(extra)
    (y_ref,) = take(1)
    z_ref = take(1)[0] if last else None
    db_refs = take(len(ts))
    if last:
        ka_out = vta_out = None
        acc_out = None
    else:
        ka_out, vta_out, acc_out = take(3)
    ka, vta, va, kk, s_ref, p_ref, acc, dbacc = refs
    cols = x_ref.shape[0]
    row = pl.program_id(0)
    count = meta_ref[0]
    place = lambda s: lax.rem(meta_ref[9] - s + cols, cols)

    @pl.when(row == 0)
    def _():
        dbacc[...] = jnp.zeros_like(dbacc)

    ones16 = jnp.ones((16, BLK), BF)
    zeros48 = jnp.zeros((48, BLK), BF)
    lane = lax.broadcasted_iota(jnp.int32, (16, BLK), 1)
    for s in range(cols):
        at = pl.ds(s * BLK, BLK)
        key = x_ref[s, 0, 1]
        val = x_ref[s, 0, 2]
        if first:
            mask = jnp.where(s * BLK + lane < count, 0.0, NEG).astype(BF)
            ka[at, :] = jnp.concatenate([key, key, mask, zeros48], 0).T
            vta[at, :] = jnp.concatenate([val, val, ones16, zeros48], 0).T
        va[0:DIM, at] = val
        va[DIM : DIM + 16, at] = ones16
        kk[:, at] = key
    if first:
        acc[...] = jnp.zeros_like(acc)
        ka_use, vta_use = ka, vta
    else:
        acc[...] = acc_in[0]
        y_ref[...] = y_in[...]
        ka_use, vta_use = ka_in.at[0], vta_in.at[0]
    if not last:
        ka_out[0] = ka_use[...]
        vta_out[0] = vta_use[...]
    sub = lax.broadcasted_iota(jnp.int32, (16, 2 * BLK), 0)
    unit = jnp.where(sub == 0, 1.0, 0.0).astype(BF)
    zero48 = jnp.zeros((48, 2 * BLK), BF)
    zero64 = jnp.zeros((64, 2 * BLK), BF)
    zero32 = jnp.zeros((32, 2 * BLK), BF)

    def scores(n, t, steps):
        b_ref = b_refs[n]
        j0 = meta_ref[1 + 2 * t]
        j1 = meta_ref[2 + 2 * t]
        q = jnp.concatenate([x_ref[j0, 0, 0], x_ref[j1, 0, 0]], 1)
        qs = q.astype(F32) * (SCALE * LOG2E)
        qhi = qs.astype(BF)
        qlo = (qs - qhi.astype(F32)).astype(BF)
        qa = jnp.concatenate([qhi, qlo, unit, zero48], 0)
        top = None
        for kb in range(steps):
            at = pl.ds(kb * 2 * BLK, 2 * BLK)
            s = jnp.dot(ka_use[at, :], qa, preferred_element_type=F32)
            bias = jnp.concatenate(
                [
                    jnp.concatenate([b_ref[0, place(2 * kb + e)], b_ref[1, place(2 * kb + e)]], 1)
                    for e in range(2)
                ],
                0,
            )
            s = s + bias
            s_ref[n, at, :] = s
            m = jnp.max(s, axis=0, keepdims=True)
            top = m if top is None else jnp.maximum(top, m)
        return j0, j1, q, top

    def weights(n, top, steps):
        o = None
        for kb in range(steps):
            at = pl.ds(kb * 2 * BLK, 2 * BLK)
            p = jnp.exp2(s_ref[n, at, :] - top)
            s_ref[n, at, :] = p
            pb = p.astype(BF)
            p_ref[n, at, :] = pb
            part = jnp.dot(va[:, at], pb, preferred_element_type=F32)
            o = part if o is None else o + part
        return o

    def middle(n, j0, j1, q, o):
        ag = jnp.concatenate([x_ref[j0, 0, 3], x_ref[j1, 0, 3]], 1).astype(F32)
        inv = 1.0 / o[DIM : DIM + 1]
        att = o[:DIM] * inv
        delta = jnp.sum(ag * att, axis=0, keepdims=True) * inv
        do = ag * inv
        dohi = do.astype(BF)
        dolo = (do - dohi.astype(F32)).astype(BF)
        d1 = delta.astype(BF).astype(F32)
        d2 = (delta - d1).astype(BF).astype(F32)
        d3 = delta - d1 - d2
        drow = jnp.where(sub == 0, -d1, jnp.where(sub == 1, -d2, jnp.where(sub == 2, -d3, 0.0)))
        doa = jnp.concatenate([dohi, dolo, drow.astype(BF), zero48], 0)
        w = jnp.concatenate(
            [
                jnp.concatenate([dohi, dolo, zero64], 0),
                jnp.concatenate([zero64, q, zero32], 0),
            ],
            1,
        )
        attb = att.astype(BF)
        y_ref[j0, 0, 1] = attb[:, :BLK]
        y_ref[j1, 0, 1] = attb[:, BLK:]
        return doa, w

    def gradients(n, kb, doa):
        at = pl.ds(kb * 2 * BLK, 2 * BLK)
        dp = jnp.dot(vta_use[at, :], doa, preferred_element_type=F32)
        ds = s_ref[n, at, :] * dp
        dsb = ds.astype(BF)
        for e in range(2):
            part = ds[e * BLK : (e + 1) * BLK]
            dbacc[n, 0, place(2 * kb + e)] += part[:, :BLK]
            dbacc[n, 1, place(2 * kb + e)] += part[:, BLK:]
        both = jnp.concatenate([p_ref[n, at, :], dsb], 1)
        return jnp.dot(kk[:, at], dsb, preferred_element_type=F32), both

    def chunks(some, steps):
        first_stage = [scores(n, ts[n], steps) for n in some]
        outs = [weights(n, f[3], steps) for n, f in zip(some, first_stage)]
        mids = [middle(n, f[0], f[1], f[2], o) for n, f, o in zip(some, first_stage, outs)]
        dqs = [None] * len(some)
        for kb in range(steps):
            at = pl.ds(kb * 2 * BLK, 2 * BLK)
            terms = []
            for i, n in enumerate(some):
                part, both = gradients(n, kb, mids[i][0])
                dqs[i] = part if dqs[i] is None else dqs[i] + part
                terms.append(lax.dot_general(both, mids[i][1], NT, preferred_element_type=F32))
            acc[at, :] += sum(terms[1:], terms[0])
        for f, dq in zip(first_stage, dqs):
            dq = (dq * SCALE).astype(BF)
            y_ref[f[0], 0, 0] = dq[:, :BLK]
            y_ref[f[1], 0, 0] = dq[:, BLK:]

    def live(steps, low, high):
        @pl.when(jnp.logical_and(count > low, count <= high))
        def _():
            for start in range(0, len(ts), 2):
                chunks(range(start, min(start + 2, len(ts))), steps)

    full = cols // 2
    live(full, (full - 1) * 2 * BLK, full * 2 * BLK)
    live(full - 1, (full - 2) * 2 * BLK, (full - 1) * 2 * BLK)
    live(full - 2, 0, (full - 2) * 2 * BLK)

    if last:
        for s in range(cols):
            a = acc[s * BLK : (s + 1) * BLK, :].T
            z_ref[s, 0, 1] = (a[0:DIM] + a[DIM : 2 * DIM]).astype(BF)
            z_ref[s, 0, 0] = (a[2 * DIM : 3 * DIM] * SCALE).astype(BF)
    else:
        acc_out[0] = acc[...]

    @pl.when(row == pl.num_programs(0) - 1)
    def _():
        for n in range(len(ts)):
            total = dbacc[n]
            if n == len(ts) - 1:
                for r_ref in r_refs:
                    total = total + r_ref[...].astype(F32)
            db_refs[n][...] = total.astype(db_refs[n].dtype)


def attend(meta, x, biases, ts, state=None, last=False, extra=()):
    first = state is None
    cols, rows = x.shape[:2]
    wide = cols * BLK
    per_row = lambda n: pl.BlockSpec((cols, 1, n, DIM, BLK), lambda r: (0, r, 0, 0, 0))
    pairs = jax.ShapeDtypeStruct((cols, rows, 2, DIM, BLK), BF)
    tile = pl.BlockSpec((2, cols, BLK, BLK), lambda r: (0, 0, 0, 0))
    flat = pl.BlockSpec((1, wide, BLK), lambda r: (r, 0, 0))
    tile_shape = (2, cols, BLK, BLK)
    flat_shape = (rows, wide, BLK)
    in_specs = [pl.BlockSpec(memory_space=pltpu.SMEM), per_row(4)] + [tile] * len(ts)
    operands = [meta, x] + [biases[t] for t in ts]
    if not first:
        in_specs += [flat, flat, flat, per_row(2)]
        operands += list(state)
    in_specs += [tile] * len(extra)
    operands += list(extra)
    out_specs = [per_row(2)] * (2 if last else 1) + [tile] * len(ts)
    out_shape = [pairs] * (2 if last else 1)
    out_shape += [jax.ShapeDtypeStruct(tile_shape, F32 if last else BF)] * len(ts)
    if not last:
        out_specs += [flat] * 3
        out_shape += [jax.ShapeDtypeStruct(flat_shape, dt) for dt in (BF, BF, F32)]
    outs = pl.pallas_call(
        functools.partial(attend_kernel, ts, first, last, len(extra)),
        grid=(rows,),
        in_specs=in_specs,
        out_specs=out_specs,
        out_shape=out_shape,
        scratch_shapes=[
            pltpu.VMEM((wide, BLK), BF),
            pltpu.VMEM((wide, BLK), BF),
            pltpu.VMEM((DIM + 16, wide), BF),
            pltpu.VMEM((DIM, wide), BF),
            pltpu.VMEM((len(ts), wide, 2 * BLK), F32),
            pltpu.VMEM((len(ts), wide, 2 * BLK), BF),
            pltpu.VMEM((wide, BLK), F32),
            pltpu.VMEM((len(ts),) + tile_shape, F32),
        ],
        compiler_params=pltpu.CompilerParams(
            vmem_limit_bytes=(18 if len(ts) > 1 else 11) * 1024 * 1024
        ),
        cost_estimate=pl.CostEstimate(
            flops=len(ts) * 2_000_000_000, bytes_accessed=8_000_000, transcendentals=0
        ),
    )(*operands)
    if last:
        return *outs[:2], dict(zip(ts, outs[2:])), None
    dbs, rest = outs[1 : 1 + len(ts)], outs[1 + len(ts) :]
    return outs[0], dict(zip(ts, dbs)), (*rest, outs[0])


VMEM_SPEC = pl.BlockSpec(memory_space=pltpu.VMEM)


def split(q, k, v, g, c, cols):
    rows = q.shape[2]
    return pl.pallas_call(
        split_kernel,
        in_specs=[VMEM_SPEC] * 5,
        out_specs=VMEM_SPEC,
        out_shape=jax.ShapeDtypeStruct((cols, rows // cols, 4, DIM, BLK), BF),
        scratch_shapes=[pltpu.VMEM((4, DIM * rows, BLK), F32)],
        compiler_params=pltpu.CompilerParams(vmem_limit_bytes=8 * 1024 * 1024),
    )(q, k, v, g, c)


def merge(y, z, g, c):
    rows = g.shape[2]
    return pl.pallas_call(
        merge_kernel,
        in_specs=[VMEM_SPEC] * 4,
        out_specs=[VMEM_SPEC] * 4,
        out_shape=[jax.ShapeDtypeStruct(g.shape, BF)] * 4,
        scratch_shapes=[pltpu.VMEM((4, DIM * rows, BLK), F32)],
        compiler_params=pltpu.CompilerParams(vmem_limit_bytes=8 * 1024 * 1024),
    )(y, z, g, c)


def shift(x, axis, n, by):
    return lax.ppermute(x, axis, [(i, (i + by) % n) for i in range(n)])


def shift_x(x, by):
    return lax.ppermute(x, "row", [(r, r // 4 * 4 + (r + by) % 4) for r in range(8)])


def swap_y(x):
    return lax.ppermute(x, "row", [(r, (r + 4) % 8) for r in range(8)])


def gather_z(own, cols):
    far = jnp.stack([own, shift(own, "col", cols, 3), shift(own, "col", cols, -3)])
    low = shift(far, "col", cols, 1)
    high = shift(far[:2], "col", cols, -1)
    return jnp.stack([own, low[0], high[1], far[1], low[1], far[2], low[2], high[0]])


def reduce_z(strip, cols, after):
    part = strip.astype(BF)
    low = shift(jnp.stack([part[1], part[4], part[6]]), "col", cols, -1).astype(F32)
    high = shift(jnp.stack([part[7], part[2]]), "col", cols, 1).astype(F32)
    left = shift((strip[3] + low[1] + high[1]).astype(BF), "col", cols, -3).astype(F32)
    right = shift((strip[5] + low[2]).astype(BF), "col", cols, 3).astype(F32)
    left, right, after = lax.optimization_barrier((left, right, after))
    return strip[0] + low[0] + high[0] + left + right, after


def body(q, k, v, g, c, pair, weight, lengths):
    cols = lax.axis_size("col")
    col = lax.axis_index("col")
    row = lax.axis_index("row")
    head = lax.axis_index("head")
    count = jnp.sum(lengths)
    away = jnp.arange(8)
    block = jnp.remainder(row // 4 + away % 2, 2) * 4 + jnp.remainder(row - away // 2, 4)
    meta = jnp.concatenate([count[None], block, col[None]]).astype(jnp.int32)

    partial = jnp.dot(
        weight.T, pair.reshape(pair.shape[0], BLK * BLK), preferred_element_type=F32
    ).reshape(HEADS, BLK, BLK)
    own = lax.dynamic_index_in_dim(partial, head, 0, keepdims=False)
    for s in range(1, HEADS):
        give = lax.dynamic_index_in_dim(
            partial, jnp.remainder(head + s, HEADS), 0, keepdims=False
        )
        own = own + shift(give, "head", HEADS, s)
    own = (own.T * LOG2E).astype(jnp.float16)

    x = split(q, k, v, g, c, cols)
    along_z = gather_z(own, cols)
    x, along_z = lax.optimization_barrier((x, along_z))
    x = lax.all_to_all(x, "col", 0, 0)
    along_y = jnp.stack([along_z, swap_y(along_z)])
    raw = {t: shift_x(along_y, t) for t in (2, 1, 3)}

    _, db, state = attend(meta, x, {2: raw[2].astype(F32)}, (2,))
    got2 = shift_x(db[2], -2)
    raw1, raw3, state = lax.optimization_barrier((raw[1], raw[3], state))
    _, db, state = attend(meta, x, {1: raw1.astype(F32), 3: raw3.astype(F32)}, (1, 3), state)
    got1, got3 = shift_x(db[1], -1), shift_x(db[3], -3)
    y, z, db, _ = attend(meta, x, {0: along_y.astype(F32)}, (0,), state, True, (got2,))

    y = lax.all_to_all(y, "col", 0, 0)
    both = db[0] + got1.astype(F32) + got3.astype(F32)
    strip = both[0] + swap_y(both[1].astype(BF)).astype(F32)
    mine, z = reduce_z(strip, cols, z)
    z = lax.all_to_all(z, "col", 0, 0)
    dq, dk, dv, dg = merge(y, z, g, c)
    mine = mine.T
    wf = weight.astype(F32)
    every = [mine] + [shift(mine, "head", HEADS, s) for s in range(1, HEADS)]
    order = jnp.remainder(head - jnp.arange(HEADS), HEADS)
    turned = jnp.take(wf, order, axis=1)
    dpair = jnp.dot(
        turned,
        jnp.stack(every).reshape(HEADS, BLK * BLK),
        precision=lax.Precision.HIGHEST,
    )
    dpair = dpair.reshape(pair.shape).astype(BF)
    return dq, dk, dv, dg, dpair


def solution(mesh):
    spec = P("head", None, "row", "col")
    pair_spec = P("head", "row", "col")
    return jax.shard_map(
        body,
        mesh=mesh,
        in_specs=(spec,) * 5 + (pair_spec, P("head", None), P()),
        out_specs=(spec,) * 4 + (pair_spec,),
        check_vma=False,
    )
```

```python
import functools
import math

import jax
import jax.numpy as jnp
from jax import lax
from jax.experimental import pallas as pl
from jax.experimental.pallas import tpu as pltpu
from jax.sharding import PartitionSpec as P

HEADS = 4
DIM = 32
BLK = 128
SCALE = DIM**-0.5
LOG2E = math.log2(math.e)
BF = jnp.bfloat16
F32 = jnp.float32
NT = (((1,), (1,)), ((), ()))
NEG = -1e9


def split_kernel(q_ref, k_ref, v_ref, g_ref, c_ref, x_ref, buf):
    cols, per = x_ref.shape[:2]
    rows = q_ref.shape[2]
    ag = (c_ref[0].astype(F32) * jax.nn.sigmoid(g_ref[0].astype(F32))).astype(BF)
    for a, value in enumerate((q_ref[0], k_ref[0], v_ref[0], ag)):
        buf[a] = value.astype(F32).reshape(DIM * rows, BLK)
    for dest in range(cols):
        for r in range(per):
            for a in range(4):
                part = buf[a, pl.ds(r * cols + dest, DIM, rows)].astype(BF)
                x_ref[dest, r, a] = part


def merge_kernel(x_ref, first_ref, second_ref, buf):
    cols, per = x_ref.shape[:2]
    rows = first_ref.shape[2]
    for src in range(cols):
        for r in range(per):
            for a in range(2):
                buf[a, pl.ds(r * cols + src, DIM, rows)] = x_ref[src, r, a].astype(F32)
    for a, out in enumerate((first_ref, second_ref)):
        out[0] = buf[a].reshape(DIM, rows, BLK).astype(BF)


def merge_gate_kernel(x_ref, g_ref, c_ref, first_ref, gate_ref, buf):
    cols, per = x_ref.shape[:2]
    rows = first_ref.shape[2]
    for src in range(cols):
        for r in range(per):
            for a in range(2):
                buf[a, pl.ds(r * cols + src, DIM, rows)] = x_ref[src, r, a].astype(F32)
    first_ref[0] = buf[0].reshape(DIM, rows, BLK).astype(BF)
    gate = jax.nn.sigmoid(g_ref[0].astype(F32))
    attended = buf[1].reshape(DIM, rows, BLK)
    gate_ref[0] = (c_ref[0].astype(F32) * attended * gate * (1.0 - gate)).astype(BF)


def attend_kernel(ts, first, last, extra, *refs):
    refs = list(refs)
    take = lambda n: [refs.pop(0) for _ in range(n)]
    meta_ref, x_ref = take(2)
    b_refs = take(len(ts))
    if first:
        ka_in = vta_in = acc_in = y_in = None
    else:
        ka_in, vta_in, acc_in, y_in = take(4)
    r_refs = take(extra)
    (y_ref,) = take(1)
    z_ref = take(1)[0] if last else None
    db_refs = take(len(ts))
    if last:
        ka_out = vta_out = None
        acc_out = None
    else:
        ka_out, vta_out, acc_out = take(3)
    ka, vta, va, kk, s_ref, p_ref, acc, dbacc = refs
    cols = x_ref.shape[0]
    row = pl.program_id(0)
    count = meta_ref[0]
    place = lambda s: lax.rem(meta_ref[9] - s + cols, cols)

    @pl.when(row == 0)
    def _():
        dbacc[...] = jnp.zeros_like(dbacc)

    ones16 = jnp.ones((16, BLK), BF)
    zeros48 = jnp.zeros((48, BLK), BF)
    lane = lax.broadcasted_iota(jnp.int32, (16, BLK), 1)
    for s in range(cols):
        at = pl.ds(s * BLK, BLK)
        key = x_ref[s, 0, 1]
        val = x_ref[s, 0, 2]
        if first:
            mask = jnp.where(s * BLK + lane < count, 0.0, NEG).astype(BF)
            ka[at, :] = jnp.concatenate([key, key, mask, zeros48], 0).T
            vta[at, :] = jnp.concatenate([val, val, ones16, zeros48], 0).T
        va[0:DIM, at] = val
        va[DIM : DIM + 16, at] = ones16
        kk[:, at] = key
    if first:
        acc[...] = jnp.zeros_like(acc)
        ka_use, vta_use = ka, vta
    else:
        acc[...] = acc_in[0]
        y_ref[...] = y_in[...]
        ka_use, vta_use = ka_in.at[0], vta_in.at[0]
    if not last:
        ka_out[0] = ka_use[...]
        vta_out[0] = vta_use[...]
    sub = lax.broadcasted_iota(jnp.int32, (16, 2 * BLK), 0)
    unit = jnp.where(sub == 0, 1.0, 0.0).astype(BF)
    zero48 = jnp.zeros((48, 2 * BLK), BF)
    zero64 = jnp.zeros((64, 2 * BLK), BF)
    zero32 = jnp.zeros((32, 2 * BLK), BF)

    def scores(n, t, steps):
        b_ref = b_refs[n]
        j0 = meta_ref[1 + 2 * t]
        j1 = meta_ref[2 + 2 * t]
        q = jnp.concatenate([x_ref[j0, 0, 0], x_ref[j1, 0, 0]], 1)
        qs = q.astype(F32) * (SCALE * LOG2E)
        qhi = qs.astype(BF)
        qlo = (qs - qhi.astype(F32)).astype(BF)
        qa = jnp.concatenate([qhi, qlo, unit, zero48], 0)
        top = None
        for kb in range(steps):
            at = pl.ds(kb * 2 * BLK, 2 * BLK)
            s = jnp.dot(ka_use[at, :], qa, preferred_element_type=F32)
            bias = jnp.concatenate(
                [
                    jnp.concatenate([b_ref[0, place(2 * kb + e)], b_ref[1, place(2 * kb + e)]], 1)
                    for e in range(2)
                ],
                0,
            )
            s = s + bias
            s_ref[n, at, :] = s
            m = jnp.max(s, axis=0, keepdims=True)
            top = m if top is None else jnp.maximum(top, m)
        return j0, j1, q, top

    def weights(n, top, steps):
        o = None
        for kb in range(steps):
            at = pl.ds(kb * 2 * BLK, 2 * BLK)
            p = jnp.exp2(s_ref[n, at, :] - top)
            s_ref[n, at, :] = p
            pb = p.astype(BF)
            p_ref[n, at, :] = pb
            part = jnp.dot(va[:, at], pb, preferred_element_type=F32)
            o = part if o is None else o + part
        return o

    def middle(n, j0, j1, q, o):
        ag = jnp.concatenate([x_ref[j0, 0, 3], x_ref[j1, 0, 3]], 1).astype(F32)
        inv = 1.0 / o[DIM : DIM + 1]
        att = o[:DIM] * inv
        delta = jnp.sum(ag * att, axis=0, keepdims=True) * inv
        do = ag * inv
        dohi = do.astype(BF)
        dolo = (do - dohi.astype(F32)).astype(BF)
        d1 = delta.astype(BF).astype(F32)
        d2 = (delta - d1).astype(BF).astype(F32)
        d3 = delta - d1 - d2
        drow = jnp.where(sub == 0, -d1, jnp.where(sub == 1, -d2, jnp.where(sub == 2, -d3, 0.0)))
        doa = jnp.concatenate([dohi, dolo, drow.astype(BF), zero48], 0)
        w = jnp.concatenate(
            [
                jnp.concatenate([dohi, dolo, zero64], 0),
                jnp.concatenate([zero64, q, zero32], 0),
            ],
            1,
        )
        attb = att.astype(BF)
        y_ref[j0, 0, 1] = attb[:, :BLK]
        y_ref[j1, 0, 1] = attb[:, BLK:]
        return doa, w

    def gradients(n, kb, doa):
        at = pl.ds(kb * 2 * BLK, 2 * BLK)
        dp = jnp.dot(vta_use[at, :], doa, preferred_element_type=F32)
        ds = s_ref[n, at, :] * dp
        dsb = ds.astype(BF)
        for e in range(2):
            part = ds[e * BLK : (e + 1) * BLK]
            dbacc[n, 0, place(2 * kb + e)] += part[:, :BLK]
            dbacc[n, 1, place(2 * kb + e)] += part[:, BLK:]
        both = jnp.concatenate([p_ref[n, at, :], dsb], 1)
        return jnp.dot(kk[:, at], dsb, preferred_element_type=F32), both

    def chunks(some, steps):
        first_stage = [scores(n, ts[n], steps) for n in some]
        outs = [weights(n, f[3], steps) for n, f in zip(some, first_stage)]
        mids = [middle(n, f[0], f[1], f[2], o) for n, f, o in zip(some, first_stage, outs)]
        dqs = [None] * len(some)
        for kb in range(steps):
            at = pl.ds(kb * 2 * BLK, 2 * BLK)
            terms = []
            for i, n in enumerate(some):
                part, both = gradients(n, kb, mids[i][0])
                dqs[i] = part if dqs[i] is None else dqs[i] + part
                terms.append(lax.dot_general(both, mids[i][1], NT, preferred_element_type=F32))
            acc[at, :] += sum(terms[1:], terms[0])
        for f, dq in zip(first_stage, dqs):
            dq = (dq * SCALE).astype(BF)
            y_ref[f[0], 0, 0] = dq[:, :BLK]
            y_ref[f[1], 0, 0] = dq[:, BLK:]

    def live(steps, low, high):
        @pl.when(jnp.logical_and(count > low, count <= high))
        def _():
            for start in range(0, len(ts), 2):
                chunks(range(start, min(start + 2, len(ts))), steps)

    full = cols // 2
    live(full, (full - 1) * 2 * BLK, full * 2 * BLK)
    live(full - 1, (full - 2) * 2 * BLK, (full - 1) * 2 * BLK)
    live(full - 2, 0, (full - 2) * 2 * BLK)

    if last:
        for s in range(cols):
            a = acc[s * BLK : (s + 1) * BLK, :].T
            z_ref[s, 0, 1] = (a[0:DIM] + a[DIM : 2 * DIM]).astype(BF)
            z_ref[s, 0, 0] = (a[2 * DIM : 3 * DIM] * SCALE).astype(BF)
    else:
        acc_out[0] = acc[...]

    @pl.when(row == pl.num_programs(0) - 1)
    def _():
        for n in range(len(ts)):
            total = dbacc[n]
            if n == len(ts) - 1:
                for r_ref in r_refs:
                    total = total + r_ref[...].astype(F32)
            db_refs[n][...] = total.astype(db_refs[n].dtype)


def attend(meta, x, biases, ts, state=None, last=False, extra=()):
    first = state is None
    cols, rows = x.shape[:2]
    wide = cols * BLK
    per_row = lambda n: pl.BlockSpec((cols, 1, n, DIM, BLK), lambda r: (0, r, 0, 0, 0))
    pairs = jax.ShapeDtypeStruct((cols, rows, 2, DIM, BLK), BF)
    tile = pl.BlockSpec((2, cols, BLK, BLK), lambda r: (0, 0, 0, 0))
    flat = pl.BlockSpec((1, wide, BLK), lambda r: (r, 0, 0))
    tile_shape = (2, cols, BLK, BLK)
    flat_shape = (rows, wide, BLK)
    in_specs = [pl.BlockSpec(memory_space=pltpu.SMEM), per_row(4)] + [tile] * len(ts)
    operands = [meta, x] + [biases[t] for t in ts]
    if not first:
        in_specs += [flat, flat, flat, per_row(2)]
        operands += list(state)
    in_specs += [tile] * len(extra)
    operands += list(extra)
    out_specs = [per_row(2)] * (2 if last else 1) + [tile] * len(ts)
    out_shape = [pairs] * (2 if last else 1)
    out_shape += [jax.ShapeDtypeStruct(tile_shape, F32 if last else BF)] * len(ts)
    if not last:
        out_specs += [flat] * 3
        out_shape += [jax.ShapeDtypeStruct(flat_shape, dt) for dt in (BF, BF, F32)]
    outs = pl.pallas_call(
        functools.partial(attend_kernel, ts, first, last, len(extra)),
        grid=(rows,),
        in_specs=in_specs,
        out_specs=out_specs,
        out_shape=out_shape,
        scratch_shapes=[
            pltpu.VMEM((wide, BLK), BF),
            pltpu.VMEM((wide, BLK), BF),
            pltpu.VMEM((DIM + 16, wide), BF),
            pltpu.VMEM((DIM, wide), BF),
            pltpu.VMEM((len(ts), wide, 2 * BLK), F32),
            pltpu.VMEM((len(ts), wide, 2 * BLK), BF),
            pltpu.VMEM((wide, BLK), F32),
            pltpu.VMEM((len(ts),) + tile_shape, F32),
        ],
        compiler_params=pltpu.CompilerParams(
            vmem_limit_bytes=(14 if len(ts) > 1 else 8) * 1024 * 1024
        ),
        cost_estimate=pl.CostEstimate(
            flops=len(ts) * 2_000_000_000, bytes_accessed=8_000_000, transcendentals=0
        ),
    )(*operands)
    if last:
        return *outs[:2], dict(zip(ts, outs[2:])), None
    dbs, rest = outs[1 : 1 + len(ts)], outs[1 + len(ts) :]
    return outs[0], dict(zip(ts, dbs)), (*rest, outs[0])


VMEM_SPEC = pl.BlockSpec(memory_space=pltpu.VMEM)


def split(q, k, v, g, c, cols):
    rows = q.shape[2]
    return pl.pallas_call(
        split_kernel,
        in_specs=[VMEM_SPEC] * 5,
        out_specs=VMEM_SPEC,
        out_shape=jax.ShapeDtypeStruct((cols, rows // cols, 4, DIM, BLK), BF),
        scratch_shapes=[pltpu.VMEM((4, DIM * rows, BLK), F32)],
        compiler_params=pltpu.CompilerParams(vmem_limit_bytes=5 * 1024 * 1024),
    )(q, k, v, g, c)


def merge(x, shape, *gates):
    rows = shape[2]
    return pl.pallas_call(
        merge_gate_kernel if gates else merge_kernel,
        in_specs=[VMEM_SPEC] * (1 + len(gates)),
        out_specs=[VMEM_SPEC] * 2,
        out_shape=[jax.ShapeDtypeStruct(shape, BF)] * 2,
        scratch_shapes=[pltpu.VMEM((2, DIM * rows, BLK), F32)],
        compiler_params=pltpu.CompilerParams(vmem_limit_bytes=5 * 1024 * 1024),
    )(x, *gates)


def shift(x, axis, n, by):
    return lax.ppermute(x, axis, [(i, (i + by) % n) for i in range(n)])


def shift_x(x, by):
    return lax.ppermute(x, "row", [(r, r // 4 * 4 + (r + by) % 4) for r in range(8)])


def swap_y(x):
    return lax.ppermute(x, "row", [(r, (r + 4) % 8) for r in range(8)])


def gather_z(own, cols):
    far = jnp.stack([own, shift(own, "col", cols, 3), shift(own, "col", cols, -3)])
    low = shift(far, "col", cols, 1)
    high = shift(far[:2], "col", cols, -1)
    return jnp.stack([own, low[0], high[1], far[1], low[1], far[2], low[2], high[0]])


def reduce_z(strip, cols, after):
    part = strip.astype(BF)
    low = shift(jnp.stack([part[1], part[4], part[6]]), "col", cols, -1).astype(F32)
    high = shift(jnp.stack([part[7], part[2]]), "col", cols, 1).astype(F32)
    left = shift((strip[3] + low[1] + high[1]).astype(BF), "col", cols, -3).astype(F32)
    right = shift((strip[5] + low[2]).astype(BF), "col", cols, 3).astype(F32)
    left, right, after = lax.optimization_barrier((left, right, after))
    return strip[0] + low[0] + high[0] + left + right, after


def body(q, k, v, g, c, pair, weight, lengths):
    cols = lax.axis_size("col")
    col = lax.axis_index("col")
    row = lax.axis_index("row")
    head = lax.axis_index("head")
    count = jnp.sum(lengths)
    away = jnp.arange(8)
    block = jnp.remainder(row // 4 + away % 2, 2) * 4 + jnp.remainder(row - away // 2, 4)
    meta = jnp.concatenate([count[None], block, col[None]]).astype(jnp.int32)

    partial = jnp.dot(
        weight.T, pair.reshape(pair.shape[0], BLK * BLK), preferred_element_type=F32
    ).reshape(HEADS, BLK, BLK)
    own = lax.dynamic_index_in_dim(partial, head, 0, keepdims=False)
    for s in range(1, HEADS):
        give = lax.dynamic_index_in_dim(
            partial, jnp.remainder(head + s, HEADS), 0, keepdims=False
        )
        own = own + shift(give, "head", HEADS, s)
    own = (own.T * LOG2E).astype(jnp.float16)

    x = split(q, k, v, g, c, cols)
    along_z = gather_z(own, cols)
    x, along_z = lax.optimization_barrier((x, along_z))
    x = lax.all_to_all(x, "col", 0, 0)
    along_y = jnp.stack([along_z, swap_y(along_z)])
    raw = {t: shift_x(along_y, t) for t in (2, 1, 3)}

    _, db, state = attend(meta, x, {2: raw[2].astype(F32)}, (2,))
    got2 = shift_x(db[2], -2)
    raw1, raw3, state = lax.optimization_barrier((raw[1], raw[3], state))
    _, db, state = attend(meta, x, {1: raw1.astype(F32), 3: raw3.astype(F32)}, (1, 3), state)
    got1, got3 = shift_x(db[1], -1), shift_x(db[3], -3)
    y, z, db, _ = attend(meta, x, {0: along_y.astype(F32)}, (0,), state, True, (got2,))

    y = lax.all_to_all(y, "col", 0, 0)
    both = db[0] + got1.astype(F32) + got3.astype(F32)
    strip = both[0] + swap_y(both[1].astype(BF)).astype(F32)
    mine, z = reduce_z(strip, cols, z)
    z = lax.all_to_all(z, "col", 0, 0)
    dq, dg = merge(y, g.shape, g, c)
    dk, dv = merge(z, g.shape)
    mine = mine.T
    wf = weight.astype(F32)
    every = [mine] + [shift(mine, "head", HEADS, s) for s in range(1, HEADS)]
    order = jnp.remainder(head - jnp.arange(HEADS), HEADS)
    turned = jnp.take(wf, order, axis=1)
    dpair = jnp.dot(
        turned,
        jnp.stack(every).reshape(HEADS, BLK * BLK),
        precision=lax.Precision.HIGHEST,
    )
    dpair = dpair.reshape(pair.shape).astype(BF)
    return dq, dk, dv, dg, dpair


def solution(mesh):
    spec = P("head", None, "row", "col")
    pair_spec = P("head", "row", "col")
    return jax.shard_map(
        body,
        mesh=mesh,
        in_specs=(spec,) * 5 + (pair_spec, P("head", None), P()),
        out_specs=(spec,) * 4 + (pair_spec,),
        check_vma=False,
    )
```

```python
import functools
import math

import jax
import jax.numpy as jnp
from jax import lax
from jax.experimental import pallas as pl
from jax.experimental.pallas import tpu as pltpu
from jax.sharding import PartitionSpec as P

HEADS = 4
DIM = 32
BLK = 128
SCALE = DIM**-0.5
LOG2E = math.log2(math.e)
BF = jnp.bfloat16
F32 = jnp.float32
NT = (((1,), (1,)), ((), ()))
NEG = -1e9


def split_kernel(q_ref, k_ref, v_ref, g_ref, c_ref, x_ref, buf):
    cols, per = x_ref.shape[:2]
    rows = q_ref.shape[2]
    ag = (c_ref[0].astype(F32) * jax.nn.sigmoid(g_ref[0].astype(F32))).astype(BF)
    for a, value in enumerate((q_ref[0], k_ref[0], v_ref[0], ag)):
        buf[a] = value.astype(F32).reshape(DIM * rows, BLK)
    for dest in range(cols):
        for r in range(per):
            for a in range(4):
                part = buf[a, pl.ds(r * cols + dest, DIM, rows)].astype(BF)
                x_ref[dest, r, a] = part


def merge_kernel(x_ref, first_ref, second_ref, buf):
    cols, per = x_ref.shape[:2]
    rows = first_ref.shape[2]
    for src in range(cols):
        for r in range(per):
            for a in range(2):
                buf[a, pl.ds(r * cols + src, DIM, rows)] = x_ref[src, r, a].astype(F32)
    for a, out in enumerate((first_ref, second_ref)):
        out[0] = buf[a].reshape(DIM, rows, BLK).astype(BF)


def merge_gate_kernel(x_ref, g_ref, c_ref, first_ref, gate_ref, buf):
    cols, per = x_ref.shape[:2]
    rows = first_ref.shape[2]
    for src in range(cols):
        for r in range(per):
            for a in range(2):
                buf[a, pl.ds(r * cols + src, DIM, rows)] = x_ref[src, r, a].astype(F32)
    first_ref[0] = buf[0].reshape(DIM, rows, BLK).astype(BF)
    gate = jax.nn.sigmoid(g_ref[0].astype(F32))
    attended = buf[1].reshape(DIM, rows, BLK)
    gate_ref[0] = (c_ref[0].astype(F32) * attended * gate * (1.0 - gate)).astype(BF)


def attend_kernel(ts, first, last, extra, *refs):
    refs = list(refs)
    take = lambda n: [refs.pop(0) for _ in range(n)]
    meta_ref, x_ref = take(2)
    b_refs = take(len(ts))
    if first:
        ka_in = vta_in = acc_in = y_in = None
    else:
        ka_in, vta_in, acc_in, y_in = take(4)
    r_refs = take(extra)
    (y_ref,) = take(1)
    z_ref = take(1)[0] if last else None
    db_refs = take(len(ts))
    ka_out, vta_out = take(2) if first and not last else (None, None)
    acc_out = None if last else take(1)[0]
    va, kk, s_ref, p_ref, acc, dbacc = refs
    cols = x_ref.shape[0]
    row = pl.program_id(0)
    count = meta_ref[0]
    place = lambda s: lax.rem(meta_ref[9] - s + cols, cols)

    @pl.when(row == 0)
    def _():
        dbacc[...] = jnp.zeros_like(dbacc)

    if first:
        ka_use, vta_use = ka_out.at[0], vta_out.at[0]
    else:
        ka_use, vta_use = ka_in.at[0], vta_in.at[0]
    ones16 = jnp.ones((16, BLK), BF)
    zeros48 = jnp.zeros((48, BLK), BF)
    lane = lax.broadcasted_iota(jnp.int32, (16, BLK), 1)
    for s in range(cols):
        at = pl.ds(s * BLK, BLK)
        key = x_ref[s, 0, 1]
        val = x_ref[s, 0, 2]
        if first:
            mask = jnp.where(s * BLK + lane < count, 0.0, NEG).astype(BF)
            ka_use[at, :] = jnp.concatenate([key, key, mask, zeros48], 0).T
            vta_use[at, :] = jnp.concatenate([val, val, ones16, zeros48], 0).T
        va[0:DIM, at] = val
        va[DIM : DIM + 16, at] = ones16
        kk[:, at] = key
    if first:
        acc[...] = jnp.zeros_like(acc)
    else:
        acc[...] = acc_in[0]
        y_ref[...] = y_in[...]
    sub = lax.broadcasted_iota(jnp.int32, (16, 2 * BLK), 0)
    unit = jnp.where(sub == 0, 1.0, 0.0).astype(BF)
    zero48 = jnp.zeros((48, 2 * BLK), BF)
    zero64 = jnp.zeros((64, 2 * BLK), BF)
    zero32 = jnp.zeros((32, 2 * BLK), BF)

    def scores(n, t, steps):
        b_ref = b_refs[n]
        j0 = meta_ref[1 + 2 * t]
        j1 = meta_ref[2 + 2 * t]
        q = jnp.concatenate([x_ref[j0, 0, 0], x_ref[j1, 0, 0]], 1)
        qs = q.astype(F32) * (SCALE * LOG2E)
        qhi = qs.astype(BF)
        qlo = (qs - qhi.astype(F32)).astype(BF)
        qa = jnp.concatenate([qhi, qlo, unit, zero48], 0)
        top = None
        for kb in range(steps):
            at = pl.ds(kb * 2 * BLK, 2 * BLK)
            s = jnp.dot(ka_use[at, :], qa, preferred_element_type=F32)
            bias = jnp.concatenate(
                [
                    jnp.concatenate([b_ref[0, place(2 * kb + e)], b_ref[1, place(2 * kb + e)]], 1)
                    for e in range(2)
                ],
                0,
            )
            s = s + bias
            s_ref[n, at, :] = s
            m = jnp.max(s, axis=0, keepdims=True)
            top = m if top is None else jnp.maximum(top, m)
        return j0, j1, q, top

    def weights(n, top, steps):
        o = None
        for kb in range(steps):
            at = pl.ds(kb * 2 * BLK, 2 * BLK)
            p = jnp.exp2(s_ref[n, at, :] - top)
            s_ref[n, at, :] = p
            pb = p.astype(BF)
            p_ref[n, at, :] = pb
            part = jnp.dot(va[:, at], pb, preferred_element_type=F32)
            o = part if o is None else o + part
        return o

    def middle(n, j0, j1, q, o):
        ag = jnp.concatenate([x_ref[j0, 0, 3], x_ref[j1, 0, 3]], 1).astype(F32)
        inv = 1.0 / o[DIM : DIM + 1]
        att = o[:DIM] * inv
        delta = jnp.sum(ag * att, axis=0, keepdims=True) * inv
        do = ag * inv
        dohi = do.astype(BF)
        dolo = (do - dohi.astype(F32)).astype(BF)
        d1 = delta.astype(BF).astype(F32)
        d2 = (delta - d1).astype(BF).astype(F32)
        d3 = delta - d1 - d2
        drow = jnp.where(sub == 0, -d1, jnp.where(sub == 1, -d2, jnp.where(sub == 2, -d3, 0.0)))
        doa = jnp.concatenate([dohi, dolo, drow.astype(BF), zero48], 0)
        w = jnp.concatenate(
            [
                jnp.concatenate([dohi, dolo, zero64], 0),
                jnp.concatenate([zero64, q, zero32], 0),
            ],
            1,
        )
        attb = att.astype(BF)
        y_ref[j0, 0, 1] = attb[:, :BLK]
        y_ref[j1, 0, 1] = attb[:, BLK:]
        return doa, w

    def gradients(n, kb, doa):
        at = pl.ds(kb * 2 * BLK, 2 * BLK)
        dp = jnp.dot(vta_use[at, :], doa, preferred_element_type=F32)
        ds = s_ref[n, at, :] * dp
        dsb = ds.astype(BF)
        for e in range(2):
            part = ds[e * BLK : (e + 1) * BLK]
            dbacc[n, 0, place(2 * kb + e)] += part[:, :BLK]
            dbacc[n, 1, place(2 * kb + e)] += part[:, BLK:]
        both = jnp.concatenate([p_ref[n, at, :], dsb], 1)
        return jnp.dot(kk[:, at], dsb, preferred_element_type=F32), both

    def chunks(some, steps):
        first_stage = [scores(n, ts[n], steps) for n in some]
        outs = [weights(n, f[3], steps) for n, f in zip(some, first_stage)]
        mids = [middle(n, f[0], f[1], f[2], o) for n, f, o in zip(some, first_stage, outs)]
        dqs = [None] * len(some)
        for kb in range(steps):
            at = pl.ds(kb * 2 * BLK, 2 * BLK)
            terms = []
            for i, n in enumerate(some):
                part, both = gradients(n, kb, mids[i][0])
                dqs[i] = part if dqs[i] is None else dqs[i] + part
                terms.append(lax.dot_general(both, mids[i][1], NT, preferred_element_type=F32))
            acc[at, :] += sum(terms[1:], terms[0])
        for f, dq in zip(first_stage, dqs):
            dq = (dq * SCALE).astype(BF)
            y_ref[f[0], 0, 0] = dq[:, :BLK]
            y_ref[f[1], 0, 0] = dq[:, BLK:]

    def live(steps, low, high):
        @pl.when(jnp.logical_and(count > low, count <= high))
        def _():
            for start in range(0, len(ts), 2):
                chunks(range(start, min(start + 2, len(ts))), steps)

    full = cols // 2
    live(full, (full - 1) * 2 * BLK, full * 2 * BLK)
    live(full - 1, (full - 2) * 2 * BLK, (full - 1) * 2 * BLK)
    live(full - 2, 0, (full - 2) * 2 * BLK)

    if last:
        for s in range(cols):
            a = acc[s * BLK : (s + 1) * BLK, :].T
            z_ref[s, 0, 1] = (a[0:DIM] + a[DIM : 2 * DIM]).astype(BF)
            z_ref[s, 0, 0] = (a[2 * DIM : 3 * DIM] * SCALE).astype(BF)
    else:
        acc_out[0] = acc[...]

    @pl.when(row == pl.num_programs(0) - 1)
    def _():
        for n in range(len(ts)):
            total = dbacc[n]
            if n == len(ts) - 1:
                for r_ref in r_refs:
                    total = total + r_ref[...].astype(F32)
            db_refs[n][...] = total.astype(db_refs[n].dtype)


def attend(meta, x, biases, ts, state=None, last=False, extra=()):
    first = state is None
    cols, rows = x.shape[:2]
    wide = cols * BLK
    per_row = lambda n: pl.BlockSpec((cols, 1, n, DIM, BLK), lambda r: (0, r, 0, 0, 0))
    pairs = jax.ShapeDtypeStruct((cols, rows, 2, DIM, BLK), BF)
    tile = pl.BlockSpec((2, cols, BLK, BLK), lambda r: (0, 0, 0, 0))
    flat = pl.BlockSpec((1, wide, BLK), lambda r: (r, 0, 0))
    tile_shape = (2, cols, BLK, BLK)
    flat_shape = (rows, wide, BLK)
    in_specs = [pl.BlockSpec(memory_space=pltpu.SMEM), per_row(4)] + [tile] * len(ts)
    operands = [meta, x] + [biases[t] for t in ts]
    if not first:
        in_specs += [flat, flat, flat, per_row(2)]
        operands += list(state)
    in_specs += [tile] * len(extra)
    operands += list(extra)
    out_specs = [per_row(2)] * (2 if last else 1) + [tile] * len(ts)
    out_shape = [pairs] * (2 if last else 1)
    out_shape += [jax.ShapeDtypeStruct(tile_shape, F32 if last else BF)] * len(ts)
    if not last:
        new = (BF, BF, F32) if first else (F32,)
        out_specs += [flat] * len(new)
        out_shape += [jax.ShapeDtypeStruct(flat_shape, dt) for dt in new]
    outs = pl.pallas_call(
        functools.partial(attend_kernel, ts, first, last, len(extra)),
        grid=(rows,),
        in_specs=in_specs,
        out_specs=out_specs,
        out_shape=out_shape,
        scratch_shapes=[
            pltpu.VMEM((DIM + 16, wide), BF),
            pltpu.VMEM((DIM, wide), BF),
            pltpu.VMEM((len(ts), wide, 2 * BLK), F32),
            pltpu.VMEM((len(ts), wide, 2 * BLK), BF),
            pltpu.VMEM((wide, BLK), F32),
            pltpu.VMEM((len(ts),) + tile_shape, F32),
        ],
        compiler_params=pltpu.CompilerParams(
            vmem_limit_bytes=(14 if len(ts) > 1 else 8) * 1024 * 1024
        ),
        cost_estimate=pl.CostEstimate(
            flops=len(ts) * 2_000_000_000, bytes_accessed=8_000_000, transcendentals=0
        ),
    )(*operands)
    if last:
        return *outs[:2], dict(zip(ts, outs[2:])), None
    dbs, rest = outs[1 : 1 + len(ts)], outs[1 + len(ts) :]
    kept = () if first else tuple(state[:2])
    return outs[0], dict(zip(ts, dbs)), (*kept, *rest, outs[0])


VMEM_SPEC = pl.BlockSpec(memory_space=pltpu.VMEM)


def split(q, k, v, g, c, cols):
    rows = q.shape[2]
    return pl.pallas_call(
        split_kernel,
        in_specs=[VMEM_SPEC] * 5,
        out_specs=VMEM_SPEC,
        out_shape=jax.ShapeDtypeStruct((cols, rows // cols, 4, DIM, BLK), BF),
        scratch_shapes=[pltpu.VMEM((4, DIM * rows, BLK), F32)],
        compiler_params=pltpu.CompilerParams(vmem_limit_bytes=5 * 1024 * 1024),
    )(q, k, v, g, c)


def merge(x, shape, *gates):
    rows = shape[2]
    return pl.pallas_call(
        merge_gate_kernel if gates else merge_kernel,
        in_specs=[VMEM_SPEC] * (1 + len(gates)),
        out_specs=[VMEM_SPEC] * 2,
        out_shape=[jax.ShapeDtypeStruct(shape, BF)] * 2,
        scratch_shapes=[pltpu.VMEM((2, DIM * rows, BLK), F32)],
        compiler_params=pltpu.CompilerParams(vmem_limit_bytes=5 * 1024 * 1024),
    )(x, *gates)


def shift(x, axis, n, by):
    return lax.ppermute(x, axis, [(i, (i + by) % n) for i in range(n)])


def shift_x(x, by):
    return lax.ppermute(x, "row", [(r, r // 4 * 4 + (r + by) % 4) for r in range(8)])


def swap_y(x):
    return lax.ppermute(x, "row", [(r, (r + 4) % 8) for r in range(8)])


def gather_z(own, cols):
    far = jnp.stack([own, shift(own, "col", cols, 3), shift(own, "col", cols, -3)])
    low = shift(far, "col", cols, 1)
    high = shift(far[:2], "col", cols, -1)
    return jnp.stack([own, low[0], high[1], far[1], low[1], far[2], low[2], high[0]])


def reduce_z(strip, cols, after):
    part = strip.astype(BF)
    low = shift(jnp.stack([part[1], part[4], part[6]]), "col", cols, -1).astype(F32)
    high = shift(jnp.stack([part[7], part[2]]), "col", cols, 1).astype(F32)
    left = shift((strip[3] + low[1] + high[1]).astype(BF), "col", cols, -3).astype(F32)
    right = shift((strip[5] + low[2]).astype(BF), "col", cols, 3).astype(F32)
    left, right, after = lax.optimization_barrier((left, right, after))
    return strip[0] + low[0] + high[0] + left + right, after


def body(q, k, v, g, c, pair, weight, lengths):
    cols = lax.axis_size("col")
    col = lax.axis_index("col")
    row = lax.axis_index("row")
    head = lax.axis_index("head")
    count = jnp.sum(lengths)
    away = jnp.arange(8)
    block = jnp.remainder(row // 4 + away % 2, 2) * 4 + jnp.remainder(row - away // 2, 4)
    meta = jnp.concatenate([count[None], block, col[None]]).astype(jnp.int32)

    partial = jnp.dot(
        weight.T, pair.reshape(pair.shape[0], BLK * BLK), preferred_element_type=F32
    ).reshape(HEADS, BLK, BLK)
    own = lax.dynamic_index_in_dim(partial, head, 0, keepdims=False)
    for s in range(1, HEADS):
        give = lax.dynamic_index_in_dim(
            partial, jnp.remainder(head + s, HEADS), 0, keepdims=False
        )
        own = own + shift(give, "head", HEADS, s)
    own = (own.T * LOG2E).astype(jnp.float16)

    x = split(q, k, v, g, c, cols)
    along_z = gather_z(own, cols)
    x, along_z = lax.optimization_barrier((x, along_z))
    x = lax.all_to_all(x, "col", 0, 0)
    along_y = jnp.stack([along_z, swap_y(along_z)])
    raw = {t: shift_x(along_y, t) for t in (2, 1, 3)}

    _, db, state = attend(meta, x, {2: raw[2].astype(F32)}, (2,))
    got2 = shift_x(db[2], -2)
    raw1, raw3, state = lax.optimization_barrier((raw[1], raw[3], state))
    _, db, state = attend(meta, x, {1: raw1.astype(F32), 3: raw3.astype(F32)}, (1, 3), state)
    got1, got3 = shift_x(db[1], -1), shift_x(db[3], -3)
    y, z, db, _ = attend(meta, x, {0: along_y.astype(F32)}, (0,), state, True, (got2,))

    y = lax.all_to_all(y, "col", 0, 0)
    both = db[0] + got1.astype(F32) + got3.astype(F32)
    strip = both[0] + swap_y(both[1].astype(BF)).astype(F32)
    mine, z = reduce_z(strip, cols, z)
    z = lax.all_to_all(z, "col", 0, 0)
    dq, dg = merge(y, g.shape, g, c)
    dk, dv = merge(z, g.shape)
    mine = mine.T
    wf = weight.astype(F32)
    every = [mine] + [shift(mine, "head", HEADS, s) for s in range(1, HEADS)]
    order = jnp.remainder(head - jnp.arange(HEADS), HEADS)
    turned = jnp.take(wf, order, axis=1)
    dpair = jnp.dot(
        turned,
        jnp.stack(every).reshape(HEADS, BLK * BLK),
        precision=lax.Precision.HIGHEST,
    )
    dpair = dpair.reshape(pair.shape).astype(BF)
    return dq, dk, dv, dg, dpair


def solution(mesh):
    spec = P("head", None, "row", "col")
    pair_spec = P("head", "row", "col")
    return jax.shard_map(
        body,
        mesh=mesh,
        in_specs=(spec,) * 5 + (pair_spec, P("head", None), P()),
        out_specs=(spec,) * 4 + (pair_spec,),
        check_vma=False,
    )
```
